32 devices in a mesh: groups: 2 (over y), replica: 2 (over core), tensor: 8 (over z, x).
Axes of the slice: x: 2, y: 2, z: 4, core: 2. Of those that a mesh axis runs over, the one named last changes fastest.
Arguments:
- acts: bfloat16 [256, 8192], P(('groups', 'replica'), 'tensor'), parts along dimension 0, may hold values from -6 to 6
- base_output_matrix: bfloat16 [8192, 8192], P('tensor'), may hold values from -0.09375 to 0.09375
- stored_down_factors: bfloat16 [256, 8192, 64], P('replica', 'tensor'), may hold values from -0.0625 to 0.0625
- stored_up_factors: bfloat16 [256, 64, 8192], P('replica', None, 'tensor'), may hold values from -0.75 to 0.75
- adapter_storage_row: int32 [256], replicated, may hold values from 0 to 255, each once
- adapter_per_block: int32 [16], P(('groups', 'replica')), parts along dimension 0, may hold values from 0 to 255, as said below
- adapter_per_token: int32 [256], P(('groups', 'replica')), parts along dimension 0, may hold values from -1 to 255, as said below
Outputs:
- projected: bfloat16 [256, 8192], P(('groups', 'replica'), 'tensor'), parts along dimension 0
The draws below stay inside these ranges and needn't reach their ends.
There are 2 independent parts, one for each index of `groups`. The reference program is written for one: setup_inputs(seed, part) draws one part's arguments, and reference() takes and returns one part's arrays. A program takes and returns all parts, laid end to end along the dimension named above; an argument that names none is the same for every part. Nothing has to cross between parts.
Inputs may be any that keep to these rules, and one draw needn't show every extreme that they name: A permutation: adapter a is stored at row adapter_storage_row[a] of stored_down_factors and stored_up_factors, so by replica adapter_storage_row[a] // 128. `adapter_per_block`: the adapter of each aligned block of 16 token rows. `adapter_per_token`: in each aligned block of 16 token rows, the first rows (one or more) hold that block's entry of adapter_per_block and the rest hold -1.
All inputs are finite; a program needn't handle non-finite values.
Results may differ from the reference program's by a relative error of at most 0.001.
Values may be sent and summed in bfloat16 or wider, within the bound.
A program may use at most 128 MiB of HBM per device.

```python
import jax
import jax.numpy as jnp
from jax import lax

MODEL_WIDTH = 8192
ADAPTER_RANK = 64
BLOCK = 16
ADAPTER_COUNT = 256
TOKENS = 128


def block_plan(key):
    block_count = TOKENS // BLOCK
    keys = jax.random.split(key, 5)
    first = jax.random.randint(keys[0], (block_count,), 0, ADAPTER_COUNT)
    second = jax.random.randint(keys[1], (block_count,), 0, ADAPTER_COUNT)
    third = jax.random.randint(keys[2], (block_count,), 0, ADAPTER_COUNT)
    picks = jnp.minimum(jnp.minimum(first, second), third)
    spot = jax.random.randint(keys[3], (), 0, block_count)
    picks = picks.at[spot].set(ADAPTER_COUNT - 1)
    counts = jax.random.randint(keys[4], (block_count,), 1, BLOCK + 1)
    counts = counts.at[(spot + 1) % block_count].set(1)
    return (picks.astype(jnp.int32), counts.astype(jnp.int32))


def draw_adapter_per_block(key, part):
    picks, counts = block_plan(key)
    return picks


def draw_adapter_per_token(key, part):
    picks, counts = block_plan(key)
    within = jnp.arange(BLOCK, dtype=jnp.int32)
    alive = within[None, :] < counts[:, None]
    return jnp.where(alive, picks[:, None], -1).reshape(-1).astype(jnp.int32)


def with_spikes(array, rng, source, target, shards_of, factor):
    def block_of(axis_at):
        return (jnp.arange(array.shape[axis_at]) // (array.shape[axis_at] // shards_of)).reshape((-1,) + (1,) * (array.ndim - 1 - axis_at))

    one_side = jax.random.permutation(rng, shards_of)[block_of(target)]
    other_side = (block_of(target) + shards_of // 2) % shards_of
    return jnp.where((block_of(source) == one_side) | (block_of(source) == other_side), factor * array, array)


def block_scale(stream_key, shape, shards, low, largest):
    gain = 1.0
    for dim, blocks in shards:
        steps = jax.random.uniform(jax.random.fold_in(jax.random.fold_in(stream_key, 6), dim), (blocks,), jnp.float32, low / len(shards), largest / len(shards))
        gain = gain * jnp.repeat(jnp.exp(steps), shape[dim] // blocks).reshape((-1,) + (1,) * (len(shape) - 1 - dim))
    return gain


def bell_draw(own_key, extent, spread, bound, shards=(), kind=jnp.bfloat16):
    gain = block_scale(own_key, extent, shards, -0.22, 0.18) if shards else 1.0
    array = jax.random.normal(own_key, extent, jnp.float32) * spread * gain
    return jnp.minimum(jnp.maximum(array, -bound), bound).astype(kind)


def gaussian_with(own_key, shape, width, most, shards, heavy, held_as=jnp.bfloat16):
    values = width * jax.random.normal(own_key, shape, jnp.float32)
    if shards:
        values = values * block_scale(own_key, shape, shards, -0.22, 0.18)
    return jnp.clip(with_spikes(values, jax.random.fold_in(own_key, 3), *heavy), -most, most).astype(held_as)


def setup_inputs(seed: int = 0, part: int = 0) -> dict:
    splits = jax.random.split(jax.random.key(seed), 8)
    part_keys = jax.random.split(jax.random.fold_in(splits[7], part), 8)
    acts = bell_draw(part_keys[0], (TOKENS, MODEL_WIDTH), 1.0, 6.0, ((0, 2), (1, 8)))
    base_output_matrix = gaussian_with(splits[1], (MODEL_WIDTH, MODEL_WIDTH), MODEL_WIDTH ** -0.5, 0.09375, ((0, 8),), (0, 1, 8, 2.0))
    stored_down_factors = bell_draw(splits[2], (ADAPTER_COUNT, MODEL_WIDTH, ADAPTER_RANK), MODEL_WIDTH ** -0.5, 0.0625, ((0, 2), (1, 8)))
    stored_up_factors = bell_draw(splits[3], (ADAPTER_COUNT, ADAPTER_RANK, MODEL_WIDTH), ADAPTER_RANK ** -0.5, 0.75, ((0, 2), (2, 8)))
    adapter_storage_row = jax.random.permutation(splits[4], ADAPTER_COUNT).astype(jnp.int32)
    adapter_per_block = draw_adapter_per_block(jax.random.fold_in(jax.random.fold_in(splits[7], part), 71), part)
    adapter_per_token = draw_adapter_per_token(jax.random.fold_in(jax.random.fold_in(splits[7], part), 71), part)
    return {"acts": acts, "base_output_matrix": base_output_matrix, "stored_down_factors": stored_down_factors, "stored_up_factors": stored_up_factors, "adapter_storage_row": adapter_storage_row, "adapter_per_block": adapter_per_block, "adapter_per_token": adapter_per_token}


def reference(acts, base_output_matrix, stored_down_factors, stored_up_factors, adapter_storage_row, adapter_per_block, adapter_per_token):
    base = jnp.dot(acts, base_output_matrix, preferred_element_type=jnp.float32)
    block_count = TOKENS // BLOCK
    stored = adapter_storage_row[adapter_per_block].astype(jnp.int32)
    blocks = acts.reshape(block_count, BLOCK, MODEL_WIDTH)
    live = (adapter_per_token >= 0).astype(jnp.float32).reshape(block_count, BLOCK, 1)

    def one_block(items):
        rows, row_identifier, alive = items
        down_result = stored_down_factors[row_identifier]
        upper_result = stored_up_factors[row_identifier].astype(jnp.float32)
        shrunk = jnp.dot(rows, down_result, preferred_element_type=jnp.float32) * alive
        return jnp.dot(shrunk, upper_result, precision=lax.Precision.HIGHEST)

    delta = lax.map(one_block, (blocks, stored, live)).reshape(TOKENS, MODEL_WIDTH)
    return (base + delta).astype(jnp.bfloat16)
```

```python
import jax
import jax.numpy as jnp
from jax import lax
from jax.sharding import PartitionSpec as P


def shards(
    acts,
    base_output_matrix,
    stored_down_factors,
    stored_up_factors,
    adapter_storage_row,
    adapter_per_block,
    adapter_per_token,
):
    tok_rows, feature_list = acts.shape
    owned = stored_down_factors.shape[0]
    block_count = adapter_per_block.shape[0]
    block_rows = tok_rows // block_count
    wanted = lax.all_gather(adapter_per_block, "replica", axis=0, tiled=True)
    every = lax.all_gather(acts, "replica", axis=0, tiled=True)
    blocks = wanted.shape[0]
    stored = adapter_storage_row[wanted]
    here = (stored // owned == lax.axis_index("replica")).astype(jnp.float32)[:, None, None]
    local = stored % owned
    shrunk_part = jnp.einsum(
        "bkf,bfr->bkr",
        every.reshape(blocks, block_rows, feature_list),
        stored_down_factors[local],
        preferred_element_type=jnp.float32,
    )
    shrunk = lax.psum(shrunk_part * here, "tensor")
    delta_all = jnp.einsum(
        "bkr,brc->bkc",
        shrunk,
        stored_up_factors[local].astype(jnp.float32),
        precision=lax.Precision.HIGHEST,
    )
    delta = lax.psum_scatter(
        delta_all.reshape(blocks * block_rows, -1), "replica", scatter_dimension=0, tiled=True
    )
    part_base = jnp.dot(acts, base_output_matrix, preferred_element_type=jnp.float32)
    base = lax.psum_scatter(part_base, "tensor", scatter_dimension=1, tiled=True)
    alive = (adapter_per_token >= 0)[:, None]
    return (base + jnp.where(alive, delta, 0.0)).astype(jnp.bfloat16)


def solution(mesh):
    placed = (
        P(("groups", "replica"), "tensor"),
        P("tensor", None),
        P("replica", "tensor", None),
        P("replica", None, "tensor"),
        P(),
        P(("groups", "replica")),
        P(("groups", "replica")),
    )
    return jax.shard_map(
        shards,
        mesh=mesh,
        in_specs=placed,
        out_specs=P(("groups", "replica"), "tensor"),
        check_vma=False,
    )
```

```python
import functools

import jax
import jax.numpy as jnp
from jax import lax
from jax.experimental import pallas as pl
from jax.experimental.pallas import tpu as pltpu
from jax.sharding import PartitionSpec as P

MESH = pl.DeviceIdType.MESH
F32 = jnp.float32
TAIL = 128
LEVELS = 32000.0
HOPS = (2, 1, 3, 0)


def pick_kernel(owned, wanted, table, acts, others, mask, down, up, shrunk, chosen, rows, down_sem, up_sem):
    me = lax.axis_index("replica")
    count = wanted.shape[0]
    half = count // 2
    stored = [table[wanted[b]] for b in range(count)]
    copies = []
    for b in range(count):
        spot = lax.rem(stored[b], owned)
        first = pltpu.make_async_copy(down.at[spot], rows.at[b], down_sem.at[b])
        second = pltpu.make_async_copy(up.at[spot], chosen.at[b], up_sem.at[b])
        copies.append((first, second))
    for first, _ in copies:
        first.start()
    for _, second in copies:
        second.start()
    step = acts.shape[0] // half
    sides = []
    for side, source in ((0, acts), (1, others)):
        parts = []
        for b in range(half):
            at = side * half + b
            copies[at][0].wait()
            part = lax.dot_general(
                source[b * step : (b + 1) * step, :],
                rows[at],
                (((1,), (1,)), ((), ())),
                preferred_element_type=F32,
            )
            parts.append(part * (lax.div(stored[at], owned) == me).astype(F32))
        sides.append(jnp.concatenate(parts, axis=0))
    shrunk[...] = jnp.concatenate(sides, axis=1) * mask[...]
    for _, second in copies:
        second.wait()


def encode(value, slot):
    width = value.shape[1]
    largest = jnp.maximum(jnp.max(jnp.abs(value), axis=1, keepdims=True), 1e-30)
    level = jnp.ceil(jnp.log2(largest))
    factor = jnp.exp2(-level) * LEVELS
    coded = jnp.round(jnp.clip(value * factor, -32767.0, 32767.0))
    slot[:, 0:width] = coded.astype(jnp.int32).astype(jnp.int16)
    slot[:, width : width + TAIL] = (
        jnp.broadcast_to(level, (value.shape[0], TAIL)).astype(jnp.int32).astype(jnp.int16)
    )


def decode(slot, width):
    level = slot[:, width : width + TAIL].astype(jnp.int32).astype(F32)[:, 0:1]
    return slot[:, 0:width].astype(jnp.int32).astype(F32) * (jnp.exp2(level) * (1.0 / LEVELS))


def main_kernel(
    acts, matrix, shrunk, chosen, out,
    weights, x_out, x_in, z_out, z_in, s_pair, s_sum, s_in, total, d_out, d_in,
    w_sem, x_send, x_recv, z_send, z_recv, s_send, s_recv, d_send, d_recv,
):
    g = lax.axis_index("groups")
    r = lax.axis_index("replica")
    t = lax.axis_index("tensor")
    z, x = lax.div(t, 2), lax.rem(t, 2)
    width = out.shape[1]
    far = [lax.rem(z + k, 4) for k in HOPS]
    pair = (g, r, 2 * z + (1 - x))
    peers = [(g, r, 2 * far[i] + x) for i in range(3)]
    twin = (g, 1 - r, t)

    loads = []
    for i in range(4):
        for j, column in enumerate((1 - x, x)):
            place = pl.multiple_of((2 * far[i] + column) * width, width)
            loads.append(
                pltpu.make_async_copy(
                    matrix.at[:, pl.ds(place, width)], weights.at[2 * i + j], w_sem.at[2 * i + j]
                )
            )
    for load in loads:
        load.start()

    barrier = pltpu.get_barrier_semaphore()
    for device in [pair, twin] + peers:
        pl.semaphore_signal(barrier, inc=1, device_id=device, device_id_type=MESH)
    pl.semaphore_wait(barrier, 5)

    def send(source, target, one, two, device):
        copy = pltpu.make_async_remote_copy(
            src_ref=source, dst_ref=target, send_sem=one, recv_sem=two,
            device_id=device, device_id_type=MESH,
        )
        copy.start()
        return copy

    def product(at):
        loads[at].wait()
        return jnp.dot(acts[...], weights[at], preferred_element_type=F32)

    s_copies = [send(shrunk, s_pair, s_send.at[3], s_recv.at[3], pair)]
    x_copies = []
    z_copies = []

    def x_step(i):
        encode(product(2 * i), x_out.at[i])
        x_copies.append(send(x_out.at[i], x_in.at[i], x_send.at[i], x_recv.at[i], pair))

    x_step(0)
    x_step(1)
    s_copies[0].wait_recv()
    s_sum[...] = shrunk[...] + s_pair[...]
    for i in range(3):
        s_copies.append(send(s_sum, s_in.at[i], s_send.at[i], s_recv.at[i], peers[i]))
    for i in range(3):
        if i < 2:
            x_step(i + 2)
        mine = product(2 * i + 1)
        x_copies[i].wait_recv()
        encode(mine + decode(x_in.at[i], width), z_out.at[i])
        z_copies.append(send(z_out.at[i], z_in.at[i], z_send.at[i], z_recv.at[i], peers[i]))
    total[...] = product(7)

    for copy in s_copies[1:]:
        copy.wait_recv()
    full = s_sum[...] + s_in[0] + s_in[1] + s_in[2]
    high = full.astype(jnp.bfloat16)
    rest = full - high.astype(F32)
    middle = rest.astype(jnp.bfloat16)
    low = (rest - middle.astype(F32)).astype(jnp.bfloat16)
    half = chosen.shape[0] // 2
    rank = chosen.shape[1]
    step = acts.shape[0] // half

    def delta(side, b):
        rows = slice(b * step, (b + 1) * step)
        lanes = slice(side * rank, (side + 1) * rank)
        three = jnp.concatenate([high[rows, lanes], middle[rows, lanes], low[rows, lanes]], axis=0)
        got = jnp.dot(three, chosen[side * half + b], preferred_element_type=F32)
        return got[0:step] + got[step : 2 * step] + got[2 * step : 3 * step]

    for b in range(half):
        d_out[b * step : (b + 1) * step, :] = delta(1, b)
    d_copy = send(d_out, d_in, d_send, d_recv, twin)
    for b in range(half):
        total[b * step : (b + 1) * step, :] += delta(0, b)
    d_copy.wait_recv()
    total[...] += d_in[...]
    x_copies[3].wait_recv()
    total[...] += decode(x_in.at[3], width)
    for i in range(2):
        z_copies[i].wait_recv()
        total[...] += decode(z_in.at[i], width)
    z_copies[2].wait_recv()
    out[...] = (total[...] + decode(z_in.at[2], width)).astype(out.dtype)
    for copy in s_copies + x_copies + z_copies + [d_copy]:
        copy.wait_send()


def kernel_shards(
    acts,
    base_output_matrix,
    stored_down_factors,
    stored_up_factors,
    adapter_storage_row,
    adapter_per_block,
    adapter_per_token,
):
    rows, features = acts.shape
    owned, _, rank = stored_down_factors.shape
    width = stored_up_factors.shape[2]
    half = adapter_per_block.shape[0]
    names = jnp.concatenate([adapter_per_block, adapter_per_token])
    other_names = lax.ppermute(names, "replica", [(0, 1), (1, 0)])
    others = lax.ppermute(acts, "replica", [(0, 1), (1, 0)])
    wanted = jnp.concatenate([adapter_per_block, other_names[:half]])
    both = jnp.stack([adapter_per_token, other_names[half:]], axis=1)
    mask = jnp.repeat((both >= 0).astype(F32), rank, axis=1)
    smem = pl.BlockSpec(memory_space=pltpu.SMEM)
    vmem = pl.BlockSpec(memory_space=pltpu.VMEM)
    anywhere = pl.BlockSpec(memory_space=pl.ANY)
    shrunk, chosen = pl.pallas_call(
        functools.partial(pick_kernel, owned),
        out_shape=[
            jax.ShapeDtypeStruct((rows, 2 * rank), F32),
            jax.ShapeDtypeStruct((2 * half, rank, width), jnp.bfloat16),
        ],
        in_specs=[smem, smem, vmem, vmem, vmem, anywhere, anywhere],
        out_specs=[vmem, vmem],
        scratch_shapes=[
            pltpu.VMEM((2 * half, rank, features), jnp.bfloat16),
            pltpu.SemaphoreType.DMA((2 * half,)),
            pltpu.SemaphoreType.DMA((2 * half,)),
        ],
        compiler_params=pltpu.CompilerParams(vmem_limit_bytes=16 * 2**20),
        name="pick",
    )(
        wanted, adapter_storage_row, acts, others, mask,
        jnp.swapaxes(stored_down_factors, 1, 2), stored_up_factors,
    )
    coded = (rows, width + TAIL)
    dma = pltpu.SemaphoreType.DMA
    return pl.pallas_call(
        main_kernel,
        out_shape=jax.ShapeDtypeStruct((rows, width), jnp.bfloat16),
        in_specs=[vmem, anywhere, vmem, vmem],
        out_specs=vmem,
        scratch_shapes=[
            pltpu.VMEM((8, features, width), jnp.bfloat16),
            pltpu.VMEM((4,) + coded, jnp.int16),
            pltpu.VMEM((4,) + coded, jnp.int16),
            pltpu.VMEM((3,) + coded, jnp.int16),
            pltpu.VMEM((3,) + coded, jnp.int16),
            pltpu.VMEM((rows, 2 * rank), F32),
            pltpu.VMEM((rows, 2 * rank), F32),
            pltpu.VMEM((3, rows, 2 * rank), F32),
            pltpu.VMEM((rows, width), F32),
            pltpu.VMEM((rows, width), F32),
            pltpu.VMEM((rows, width), F32),
            dma((8,)), dma((4,)), dma((4,)), dma((3,)), dma((3,)), dma((4,)), dma((4,)), dma, dma,
        ],
        compiler_params=pltpu.CompilerParams(
            collective_id=0, has_side_effects=True, vmem_limit_bytes=40 * 2**20
        ),
        name="main",
    )(acts, base_output_matrix, shrunk, chosen)


def shards(
    acts,
    base_output_matrix,
    stored_down_factors,
    stored_up_factors,
    adapter_storage_row,
    adapter_per_block,
    adapter_per_token,
):
    tok_rows, feature_list = acts.shape
    owned = stored_down_factors.shape[0]
    block_count = adapter_per_block.shape[0]
    block_rows = tok_rows // block_count
    wanted = lax.all_gather(adapter_per_block, "replica", axis=0, tiled=True)
    every = lax.all_gather(acts, "replica", axis=0, tiled=True)
    blocks = wanted.shape[0]
    stored = adapter_storage_row[wanted]
    here = (stored // owned == lax.axis_index("replica")).astype(jnp.float32)[:, None, None]
    local = stored % owned
    shrunk_part = jnp.einsum(
        "bkf,bfr->bkr",
        every.reshape(blocks, block_rows, feature_list),
        stored_down_factors[local],
        preferred_element_type=jnp.float32,
    )
    shrunk = lax.psum(shrunk_part * here, "tensor")
    delta_all = jnp.einsum(
        "bkr,brc->bkc",
        shrunk,
        stored_up_factors[local].astype(jnp.float32),
        precision=lax.Precision.HIGHEST,
    )
    delta = lax.psum_scatter(
        delta_all.reshape(blocks * block_rows, -1), "replica", scatter_dimension=0, tiled=True
    )
    part_base = jnp.dot(acts, base_output_matrix, preferred_element_type=jnp.float32)
    base = lax.psum_scatter(part_base, "tensor", scatter_dimension=1, tiled=True)
    alive = (adapter_per_token >= 0)[:, None]
    return (base + jnp.where(alive, delta, 0.0)).astype(jnp.bfloat16)


def solution(mesh):
    placed = (
        P(("groups", "replica"), "tensor"),
        P("tensor", None),
        P("replica", "tensor", None),
        P("replica", None, "tensor"),
        P(),
        P(("groups", "replica")),
        P(("groups", "replica")),
    )
    fits = mesh.shape["tensor"] == 8 and mesh.shape["replica"] == 2
    return jax.shard_map(
        kernel_shards if fits else shards,
        mesh=mesh,
        in_specs=placed,
        out_specs=P(("groups", "replica"), "tensor"),
        check_vma=False,
    )
```

```python
import functools

import jax
import jax.numpy as jnp
from jax import lax
from jax.experimental import pallas as pl
from jax.experimental.pallas import tpu as pltpu
from jax.sharding import PartitionSpec as P

MESH = pl.DeviceIdType.MESH
F32 = jnp.float32
TAIL = 128
LEVELS = 32000.0
HOPS = (2, 1, 3, 0)


def pick_kernel(owned, wanted, other_wanted, table, acts, others, down, up, shrunk, chosen, rows, down_sem, up_sem):
    me = lax.axis_index("replica")
    half = wanted.shape[0]
    count = 2 * half
    stored = [table[wanted[b]] for b in range(half)]
    stored += [table[other_wanted[b]] for b in range(half)]
    copies = []
    for b in range(count):
        spot = lax.rem(stored[b], owned)
        first = pltpu.make_async_copy(down.at[spot], rows.at[b], down_sem.at[b])
        second = pltpu.make_async_copy(up.at[spot], chosen.at[b], up_sem.at[b])
        copies.append((first, second))
    for first, _ in copies:
        first.start()
    for _, second in copies:
        second.start()
    step = acts.shape[0] // half
    sides = []
    for side, source in ((0, acts), (1, others)):
        parts = []
        for b in range(half):
            at = side * half + b
            copies[at][0].wait()
            part = lax.dot_general(
                source[b * step : (b + 1) * step, :],
                rows[at],
                (((1,), (1,)), ((), ())),
                preferred_element_type=F32,
            )
            parts.append(part * (lax.div(stored[at], owned) == me).astype(F32))
        sides.append(jnp.concatenate(parts, axis=0))
    shrunk[...] = jnp.concatenate(sides, axis=1)
    for _, second in copies:
        second.wait()


def encode(value, slot):
    width = value.shape[1]
    largest = jnp.maximum(jnp.max(jnp.abs(value), axis=1, keepdims=True), 1e-30)
    level = jnp.ceil(jnp.log2(largest))
    factor = jnp.exp2(-level) * LEVELS
    coded = jnp.round(jnp.clip(value * factor, -32767.0, 32767.0))
    slot[:, 0:width] = coded.astype(jnp.int32).astype(jnp.int16)
    slot[:, width : width + TAIL] = (
        jnp.broadcast_to(level, (value.shape[0], TAIL)).astype(jnp.int32).astype(jnp.int16)
    )


def decode(slot, width):
    level = slot[:, width : width + TAIL].astype(jnp.int32).astype(F32)[:, 0:1]
    return slot[:, 0:width].astype(jnp.int32).astype(F32) * (jnp.exp2(level) * (1.0 / LEVELS))


def main_kernel(
    acts, matrix, shrunk, chosen, names, out,
    weights, x_out, x_in, z_out, z_in, s_pair, s_sum, s_in, total, d_out, d_in,
    w_sem, x_send, x_recv, z_send, z_recv, s_send, s_recv, d_send, d_recv,
):
    g = lax.axis_index("groups")
    r = lax.axis_index("replica")
    t = lax.axis_index("tensor")
    z, x = lax.div(t, 2), lax.rem(t, 2)
    width = out.shape[1]
    far = [lax.rem(z + k, 4) for k in HOPS]
    pair = (g, r, 2 * z + (1 - x))
    peers = [(g, r, 2 * far[i] + x) for i in range(3)]
    twin = (g, 1 - r, t)

    loads = []
    for i in range(4):
        for j, column in enumerate((1 - x, x)):
            place = pl.multiple_of((2 * far[i] + column) * width, width)
            loads.append(
                pltpu.make_async_copy(
                    matrix.at[:, pl.ds(place, width)], weights.at[2 * i + j], w_sem.at[2 * i + j]
                )
            )
    for load in loads:
        load.start()

    barrier = pltpu.get_barrier_semaphore()
    for device in [pair, twin] + peers:
        pl.semaphore_signal(barrier, inc=1, device_id=device, device_id_type=MESH)
    pl.semaphore_wait(barrier, 5)

    def send(source, target, one, two, device):
        copy = pltpu.make_async_remote_copy(
            src_ref=source, dst_ref=target, send_sem=one, recv_sem=two,
            device_id=device, device_id_type=MESH,
        )
        copy.start()
        return copy

    def product(at):
        loads[at].wait()
        return jnp.dot(acts[...], weights[at], preferred_element_type=F32)

    s_copies = [send(shrunk, s_pair, s_send.at[3], s_recv.at[3], pair)]
    x_copies = []
    z_copies = []

    def x_step(i):
        encode(product(2 * i), x_out.at[i])
        x_copies.append(send(x_out.at[i], x_in.at[i], x_send.at[i], x_recv.at[i], pair))

    x_step(0)
    x_step(1)
    s_copies[0].wait_recv()
    s_sum[...] = shrunk[...] + s_pair[...]
    for i in range(3):
        s_copies.append(send(s_sum, s_in.at[i], s_send.at[i], s_recv.at[i], peers[i]))
    for i in range(3):
        if i < 2:
            x_step(i + 2)
        mine = product(2 * i + 1)
        x_copies[i].wait_recv()
        encode(mine + decode(x_in.at[i], width), z_out.at[i])
        z_copies.append(send(z_out.at[i], z_in.at[i], z_send.at[i], z_recv.at[i], peers[i]))
    total[...] = product(7)

    for copy in s_copies[1:]:
        copy.wait_recv()
    full = s_sum[...] + s_in[0] + s_in[1] + s_in[2]
    high = full.astype(jnp.bfloat16)
    rest = full - high.astype(F32)
    middle = rest.astype(jnp.bfloat16)
    low = (rest - middle.astype(F32)).astype(jnp.bfloat16)
    half = chosen.shape[0] // 2
    rank = chosen.shape[1]
    step = acts.shape[0] // half

    def delta(side, b):
        rows = slice(b * step, (b + 1) * step)
        lanes = slice(side * rank, (side + 1) * rank)
        three = jnp.concatenate([high[rows, lanes], middle[rows, lanes], low[rows, lanes]], axis=0)
        got = jnp.dot(three, chosen[side * half + b], preferred_element_type=F32)
        return got[0:step] + got[step : 2 * step] + got[2 * step : 3 * step]

    for b in range(half):
        d_out[b * step : (b + 1) * step, :] = delta(1, b)
    d_copy = send(d_out, d_in, d_send, d_recv, twin)
    count = acts.shape[0]
    same = lax.broadcasted_iota(jnp.int32, (count, count), 0) == lax.broadcasted_iota(
        jnp.int32, (count, count), 1
    )
    named = jnp.broadcast_to((names[...] >= 0).astype(F32), (count, count))
    alive = jnp.sum(jnp.where(same, named, 0.0), axis=1, keepdims=True)
    own = jnp.concatenate([delta(0, b) for b in range(half)], axis=0)
    d_copy.wait_recv()
    total[...] += (own + d_in[...]) * alive
    x_copies[3].wait_recv()
    total[...] += decode(x_in.at[3], width)
    for i in range(2):
        z_copies[i].wait_recv()
        total[...] += decode(z_in.at[i], width)
    z_copies[2].wait_recv()
    out[...] = (total[...] + decode(z_in.at[2], width)).astype(out.dtype)
    for copy in s_copies + x_copies + z_copies + [d_copy]:
        copy.wait_send()


def kernel_shards(
    acts,
    base_output_matrix,
    stored_down_factors,
    stored_up_factors,
    adapter_storage_row,
    adapter_per_block,
    adapter_per_token,
):
    rows, features = acts.shape
    owned, _, rank = stored_down_factors.shape
    width = stored_up_factors.shape[2]
    half = adapter_per_block.shape[0]
    other_blocks = lax.ppermute(adapter_per_block, "replica", [(0, 1), (1, 0)])
    others = lax.ppermute(acts, "replica", [(0, 1), (1, 0)])
    smem = pl.BlockSpec(memory_space=pltpu.SMEM)
    vmem = pl.BlockSpec(memory_space=pltpu.VMEM)
    anywhere = pl.BlockSpec(memory_space=pl.ANY)
    shrunk, chosen = pl.pallas_call(
        functools.partial(pick_kernel, owned),
        out_shape=[
            jax.ShapeDtypeStruct((rows, 2 * rank), F32),
            jax.ShapeDtypeStruct((2 * half, rank, width), jnp.bfloat16),
        ],
        in_specs=[smem, smem, smem, vmem, vmem, anywhere, anywhere],
        out_specs=[vmem, vmem],
        scratch_shapes=[
            pltpu.VMEM((2 * half, rank, features), jnp.bfloat16),
            pltpu.SemaphoreType.DMA((2 * half,)),
            pltpu.SemaphoreType.DMA((2 * half,)),
        ],
        compiler_params=pltpu.CompilerParams(vmem_limit_bytes=50 * 2**20),
        name="pick",
    )(
        adapter_per_block, other_blocks, adapter_storage_row, acts, others,
        jnp.swapaxes(stored_down_factors, 1, 2), stored_up_factors,
    )
    coded = (rows, width + TAIL)
    dma = pltpu.SemaphoreType.DMA
    return pl.pallas_call(
        main_kernel,
        out_shape=jax.ShapeDtypeStruct((rows, width), jnp.bfloat16),
        in_specs=[vmem, anywhere, vmem, vmem, vmem],
        out_specs=vmem,
        scratch_shapes=[
            pltpu.VMEM((8, features, width), jnp.bfloat16),
            pltpu.VMEM((4,) + coded, jnp.int16),
            pltpu.VMEM((4,) + coded, jnp.int16),
            pltpu.VMEM((3,) + coded, jnp.int16),
            pltpu.VMEM((3,) + coded, jnp.int16),
            pltpu.VMEM((rows, 2 * rank), F32),
            pltpu.VMEM((rows, 2 * rank), F32),
            pltpu.VMEM((3, rows, 2 * rank), F32),
            pltpu.VMEM((rows, width), F32),
            pltpu.VMEM((rows, width), F32),
            pltpu.VMEM((rows, width), F32),
            dma((8,)), dma((4,)), dma((4,)), dma((3,)), dma((3,)), dma((4,)), dma((4,)), dma, dma,
        ],
        compiler_params=pltpu.CompilerParams(
            collective_id=0, has_side_effects=True, vmem_limit_bytes=50 * 2**20
        ),
        name="main",
    )(acts, base_output_matrix, shrunk, chosen, adapter_per_token.reshape(1, rows))


def shards(
    acts,
    base_output_matrix,
    stored_down_factors,
    stored_up_factors,
    adapter_storage_row,
    adapter_per_block,
    adapter_per_token,
):
    tok_rows, feature_list = acts.shape
    owned = stored_down_factors.shape[0]
    block_count = adapter_per_block.shape[0]
    block_rows = tok_rows // block_count
    wanted = lax.all_gather(adapter_per_block, "replica", axis=0, tiled=True)
    every = lax.all_gather(acts, "replica", axis=0, tiled=True)
    blocks = wanted.shape[0]
    stored = adapter_storage_row[wanted]
    here = (stored // owned == lax.axis_index("replica")).astype(jnp.float32)[:, None, None]
    local = stored % owned
    shrunk_part = jnp.einsum(
        "bkf,bfr->bkr",
        every.reshape(blocks, block_rows, feature_list),
        stored_down_factors[local],
        preferred_element_type=jnp.float32,
    )
    shrunk = lax.psum(shrunk_part * here, "tensor")
    delta_all = jnp.einsum(
        "bkr,brc->bkc",
        shrunk,
        stored_up_factors[local].astype(jnp.float32),
        precision=lax.Precision.HIGHEST,
    )
    delta = lax.psum_scatter(
        delta_all.reshape(blocks * block_rows, -1), "replica", scatter_dimension=0, tiled=True
    )
    part_base = jnp.dot(acts, base_output_matrix, preferred_element_type=jnp.float32)
    base = lax.psum_scatter(part_base, "tensor", scatter_dimension=1, tiled=True)
    alive = (adapter_per_token >= 0)[:, None]
    return (base + jnp.where(alive, delta, 0.0)).astype(jnp.bfloat16)


def solution(mesh):
    placed = (
        P(("groups", "replica"), "tensor"),
        P("tensor", None),
        P("replica", "tensor", None),
        P("replica", None, "tensor"),
        P(),
        P(("groups", "replica")),
        P(("groups", "replica")),
    )
    fits = mesh.shape["tensor"] == 8 and mesh.shape["replica"] == 2
    return jax.shard_map(
        kernel_shards if fits else shards,
        mesh=mesh,
        in_specs=placed,
        out_specs=P(("groups", "replica"), "tensor"),
        check_vma=False,
    )
```

```python
import functools

import jax
import jax.numpy as jnp
from jax import lax
from jax.experimental import pallas as pl
from jax.experimental.pallas import tpu as pltpu
from jax.sharding import PartitionSpec as P

MESH = pl.DeviceIdType.MESH
F32 = jnp.float32
TAIL = 128
LEVELS = 32000.0
ROWS = 16


def pick_kernel(owned, wanted, other_wanted, table, acts, others, down, up, shrunk, chosen, rows, down_sem, up_sem):
    me = lax.axis_index("replica")
    half = wanted.shape[0]
    count = 2 * half
    stored = [table[wanted[b]] for b in range(half)]
    stored += [table[other_wanted[b]] for b in range(half)]
    copies = []
    for b in range(count):
        spot = lax.rem(stored[b], owned)
        first = pltpu.make_async_copy(down.at[spot], rows.at[b], down_sem.at[b])
        second = pltpu.make_async_copy(up.at[spot], chosen.at[b], up_sem.at[b])
        copies.append((first, second))
    for first, _ in copies:
        first.start()
    for _, second in copies:
        second.start()
    step = acts.shape[0] // half
    sides = []
    for side, source in ((0, acts), (1, others)):
        parts = []
        for b in range(half):
            at = side * half + b
            copies[at][0].wait()
            part = lax.dot_general(
                source[b * step : (b + 1) * step, :],
                rows[at],
                (((1,), (1,)), ((), ())),
                preferred_element_type=F32,
            )
            parts.append(part * (lax.div(stored[at], owned) == me).astype(F32))
        sides.append(jnp.concatenate(parts, axis=0))
    shrunk[...] = jnp.concatenate(sides, axis=1)
    for _, second in copies:
        second.wait()


def encode(value, slot):
    count, width = value.shape
    largest = jnp.maximum(jnp.max(jnp.abs(value), axis=1, keepdims=True), 1e-30)
    level = jnp.ceil(jnp.log2(largest) * 4.0)
    factor = jnp.exp2(level * -0.25) * LEVELS
    coded = jnp.round(jnp.clip(value * factor, -32767.0, 32767.0))
    coded = coded.astype(jnp.int32).astype(jnp.int16)
    for i in range(count // ROWS):
        slot[:, i * width : (i + 1) * width] = coded[i * ROWS : (i + 1) * ROWS, :]
    row = jnp.sum(jnp.where(diagonal(count), level, 0.0), axis=0, keepdims=True)
    tail = count // ROWS * width
    slot[:, tail : tail + TAIL] = (
        jnp.broadcast_to(row, (ROWS, TAIL)).astype(jnp.int32).astype(jnp.int16)
    )


def diagonal(count):
    shape = (count, TAIL)
    return lax.broadcasted_iota(jnp.int32, shape, 0) == lax.broadcasted_iota(jnp.int32, shape, 1)


def decode(slot, width):
    folds = slot.shape[1] // width
    tail = folds * width
    row = slot[:, tail : tail + TAIL].astype(jnp.int32).astype(F32)[0:1, :]
    count = folds * ROWS
    level = jnp.sum(
        jnp.where(diagonal(count), jnp.broadcast_to(row, (count, TAIL)), 0.0), axis=1, keepdims=True
    )
    values = jnp.concatenate(
        [slot[:, i * width : (i + 1) * width].astype(jnp.int32).astype(F32) for i in range(folds)],
        axis=0,
    )
    return values * (jnp.exp2(level * 0.25) * (1.0 / LEVELS))


def main_kernel(*refs):
    z = lax.div(lax.axis_index("tensor"), 2)
    edge = jnp.logical_or(z == 0, z == 3)

    @pl.when(edge)
    def _():
        run(True, z, *refs)

    @pl.when(jnp.logical_not(edge))
    def _():
        run(False, z, *refs)


def run(
    edge, z,
    acts, matrix, shrunk, chosen, names, out,
    weights, x_out, x_in, z_out, z_in, s_pair, s_sum, s_in, total, d_out, d_in,
    w_sem, x_send, x_recv, z_send, z_recv, s_send, s_recv, d_send, d_recv,
):
    g = lax.axis_index("groups")
    r = lax.axis_index("replica")
    t = lax.axis_index("tensor")
    x = lax.rem(t, 2)
    width = out.shape[1]
    if edge:
        near = 1 + lax.div(z, 3)
        order = [3 - near, 3 - z, near, z]
        hops = [near, near, near]
        slots = [0, 1, 2]
    else:
        near = 3 * (z - 1)
        order = [near, 3 - z, 3 - near, z]
        hops = [near, 3 - z, 3 - near]
        slots = [0, 3, 1]

    def peer(at):
        return (g, r, 2 * at + x)

    pair = (g, r, 2 * z + (1 - x))
    twin = (g, 1 - r, t)
    peers = [peer(lax.rem(z + k, 4)) for k in (1, 2, 3)]

    loads = []
    for i in range(4):
        for j, column in enumerate((1 - x, x)):
            place = pl.multiple_of((2 * order[i] + column) * width, width)
            loads.append(
                pltpu.make_async_copy(
                    matrix.at[:, pl.ds(place, width)], weights.at[2 * i + j], w_sem.at[2 * i + j]
                )
            )
    for load in loads:
        load.start()

    barrier = pltpu.get_barrier_semaphore()
    for device in [pair, twin] + peers:
        pl.semaphore_signal(barrier, inc=1, device_id=device, device_id_type=MESH)
    pl.semaphore_wait(barrier, 5)

    def remote(source, target, one, two, device):
        return pltpu.make_async_remote_copy(
            src_ref=source, dst_ref=target, send_sem=one, recv_sem=two,
            device_id=device, device_id_type=MESH,
        )

    def send(*what):
        copy = remote(*what)
        copy.start()
        return copy

    def product(at):
        loads[at].wait()
        return jnp.dot(acts[...], weights[at], preferred_element_type=F32)

    def arrived(slot):
        remote(z_out.at[0], z_in.at[slot], z_send.at[0], z_recv.at[slot], peers[0]).wait_recv()
        return decode(z_in.at[slot], width)

    s_copies = [send(shrunk, s_pair, s_send.at[3], s_recv.at[3], pair)]
    x_copies = []
    z_copies = []

    def x_step(i):
        encode(product(2 * i), x_out.at[i])
        x_copies.append(send(x_out.at[i], x_in.at[i], x_send.at[i], x_recv.at[i], pair))

    x_step(0)
    x_step(1)
    s_copies[0].wait_recv()
    s_sum[...] = shrunk[...] + s_pair[...]
    for i in range(3):
        s_copies.append(send(s_sum, s_in.at[i], s_send.at[i], s_recv.at[i], peers[i]))
    for i in range(3):
        if i < 2:
            x_step(i + 2)
        mine = product(2 * i + 1)
        x_copies[i].wait_recv()
        mine = mine + decode(x_in.at[i], width)
        if not edge and i:
            mine = mine + arrived(i - 1)
        encode(mine, z_out.at[i])
        z_copies.append(
            send(z_out.at[i], z_in.at[slots[i]], z_send.at[i], z_recv.at[slots[i]], peer(hops[i]))
        )
    total[...] = product(7)

    for copy in s_copies[1:]:
        copy.wait_recv()
    full = s_sum[...] + s_in[0] + s_in[1] + s_in[2]
    high = full.astype(jnp.bfloat16)
    rest = full - high.astype(F32)
    middle = rest.astype(jnp.bfloat16)
    low = (rest - middle.astype(F32)).astype(jnp.bfloat16)
    half = chosen.shape[0] // 2
    rank = chosen.shape[1]
    count = acts.shape[0]
    step = count // half

    def delta(side, b):
        rows = slice(b * step, (b + 1) * step)
        lanes = slice(side * rank, (side + 1) * rank)
        three = jnp.concatenate([high[rows, lanes], middle[rows, lanes], low[rows, lanes]], axis=0)
        got = jnp.dot(three, chosen[side * half + b], preferred_element_type=F32)
        return got[0:step] + got[step : 2 * step] + got[2 * step : 3 * step]

    for b in range(half):
        d_out[b * step : (b + 1) * step, :] = delta(1, b)
    d_copy = send(d_out, d_in, d_send, d_recv, twin)
    same = lax.broadcasted_iota(jnp.int32, (count, count), 0) == lax.broadcasted_iota(
        jnp.int32, (count, count), 1
    )
    named = jnp.broadcast_to((names[...] >= 0).astype(F32), (count, count))
    alive = jnp.sum(jnp.where(same, named, 0.0), axis=1, keepdims=True)
    own = jnp.concatenate([delta(0, b) for b in range(half)], axis=0)
    d_copy.wait_recv()
    total[...] += (own + d_in[...]) * alive
    x_copies[3].wait_recv()
    total[...] += decode(x_in.at[3], width)
    if edge:
        total[...] += arrived(0)
        last = 1
    else:
        total[...] += arrived(2)
        last = 3
    out[...] = (total[...] + arrived(last)).astype(out.dtype)
    for copy in s_copies + x_copies + z_copies + [d_copy]:
        copy.wait_send()


def kernel_shards(
    acts,
    base_output_matrix,
    stored_down_factors,
    stored_up_factors,
    adapter_storage_row,
    adapter_per_block,
    adapter_per_token,
):
    rows, features = acts.shape
    owned, _, rank = stored_down_factors.shape
    width = stored_up_factors.shape[2]
    half = adapter_per_block.shape[0]
    other_blocks = lax.ppermute(adapter_per_block, "replica", [(0, 1), (1, 0)])
    others = lax.ppermute(acts, "replica", [(0, 1), (1, 0)])
    smem = pl.BlockSpec(memory_space=pltpu.SMEM)
    vmem = pl.BlockSpec(memory_space=pltpu.VMEM)
    anywhere = pl.BlockSpec(memory_space=pl.ANY)
    shrunk, chosen = pl.pallas_call(
        functools.partial(pick_kernel, owned),
        out_shape=[
            jax.ShapeDtypeStruct((rows, 2 * rank), F32),
            jax.ShapeDtypeStruct((2 * half, rank, width), jnp.bfloat16),
        ],
        in_specs=[smem, smem, smem, vmem, vmem, anywhere, anywhere],
        out_specs=[vmem, vmem],
        scratch_shapes=[
            pltpu.VMEM((2 * half, rank, features), jnp.bfloat16),
            pltpu.SemaphoreType.DMA((2 * half,)),
            pltpu.SemaphoreType.DMA((2 * half,)),
        ],
        compiler_params=pltpu.CompilerParams(vmem_limit_bytes=50 * 2**20),
        name="pick",
    )(
        adapter_per_block, other_blocks, adapter_storage_row, acts, others,
        jnp.swapaxes(stored_down_factors, 1, 2), stored_up_factors,
    )
    coded = (ROWS, rows // ROWS * width + TAIL)
    dma = pltpu.SemaphoreType.DMA
    return pl.pallas_call(
        main_kernel,
        out_shape=jax.ShapeDtypeStruct((rows, width), jnp.bfloat16),
        in_specs=[vmem, anywhere, vmem, vmem, vmem],
        out_specs=vmem,
        scratch_shapes=[
            pltpu.VMEM((8, features, width), jnp.bfloat16),
            pltpu.VMEM((4,) + coded, jnp.int16),
            pltpu.VMEM((4,) + coded, jnp.int16),
            pltpu.VMEM((3,) + coded, jnp.int16),
            pltpu.VMEM((4,) + coded, jnp.int16),
            pltpu.VMEM((rows, 2 * rank), F32),
            pltpu.VMEM((rows, 2 * rank), F32),
            pltpu.VMEM((3, rows, 2 * rank), F32),
            pltpu.VMEM((rows, width), F32),
            pltpu.VMEM((rows, width), F32),
            pltpu.VMEM((rows, width), F32),
            dma((8,)), dma((4,)), dma((4,)), dma((3,)), dma((4,)), dma((4,)), dma((4,)), dma, dma,
        ],
        compiler_params=pltpu.CompilerParams(
            collective_id=0, has_side_effects=True, vmem_limit_bytes=50 * 2**20
        ),
        name="main",
    )(acts, base_output_matrix, shrunk, chosen, adapter_per_token.reshape(1, rows))


def shards(
    acts,
    base_output_matrix,
    stored_down_factors,
    stored_up_factors,
    adapter_storage_row,
    adapter_per_block,
    adapter_per_token,
):
    tok_rows, feature_list = acts.shape
    owned = stored_down_factors.shape[0]
    block_count = adapter_per_block.shape[0]
    block_rows = tok_rows // block_count
    wanted = lax.all_gather(adapter_per_block, "replica", axis=0, tiled=True)
    every = lax.all_gather(acts, "replica", axis=0, tiled=True)
    blocks = wanted.shape[0]
    stored = adapter_storage_row[wanted]
    here = (stored // owned == lax.axis_index("replica")).astype(jnp.float32)[:, None, None]
    local = stored % owned
    shrunk_part = jnp.einsum(
        "bkf,bfr->bkr",
        every.reshape(blocks, block_rows, feature_list),
        stored_down_factors[local],
        preferred_element_type=jnp.float32,
    )
    shrunk = lax.psum(shrunk_part * here, "tensor")
    delta_all = jnp.einsum(
        "bkr,brc->bkc",
        shrunk,
        stored_up_factors[local].astype(jnp.float32),
        precision=lax.Precision.HIGHEST,
    )
    delta = lax.psum_scatter(
        delta_all.reshape(blocks * block_rows, -1), "replica", scatter_dimension=0, tiled=True
    )
    part_base = jnp.dot(acts, base_output_matrix, preferred_element_type=jnp.float32)
    base = lax.psum_scatter(part_base, "tensor", scatter_dimension=1, tiled=True)
    alive = (adapter_per_token >= 0)[:, None]
    return (base + jnp.where(alive, delta, 0.0)).astype(jnp.bfloat16)


def solution(mesh):
    placed = (
        P(("groups", "replica"), "tensor"),
        P("tensor", None),
        P("replica", "tensor", None),
        P("replica", None, "tensor"),
        P(),
        P(("groups", "replica")),
        P(("groups", "replica")),
    )
    fits = mesh.shape["tensor"] == 8 and mesh.shape["replica"] == 2
    return jax.shard_map(
        kernel_shards if fits else shards,
        mesh=mesh,
        in_specs=placed,
        out_specs=P(("groups", "replica"), "tensor"),
        check_vma=False,
    )
```

```python
import functools

import jax
import jax.numpy as jnp
from jax import lax
from jax.experimental import pallas as pl
from jax.experimental.pallas import tpu as pltpu
from jax.sharding import PartitionSpec as P

MESH = pl.DeviceIdType.MESH
F32 = jnp.float32
TAIL = 128
LEVELS = 32000.0
ROWS = 16
USED = (0, 2, 4, 1, 6, 3, 5, 7)
AHEAD = 2


def pick_kernel(
    owned, wanted_in, other_in, table_in, acts_in, others, down, up, shrunk, chosen,
    wanted, other_wanted, table, acts, rows, in_sem, down_sem, up_sem,
):
    inputs = [
        pltpu.make_async_copy(source, target, in_sem.at[i])
        for i, (source, target) in enumerate(
            ((wanted_in, wanted), (other_in, other_wanted), (table_in, table), (acts_in, acts))
        )
    ]
    for copy in inputs:
        copy.start()
    for copy in inputs[:3]:
        copy.wait()
    me = lax.axis_index("replica")
    half = wanted.shape[0]
    count = 2 * half
    stored = [table[wanted[b]] for b in range(half)]
    stored += [table[other_wanted[b]] for b in range(half)]
    copies = []
    for b in range(count):
        spot = lax.rem(stored[b], owned)
        first = pltpu.make_async_copy(down.at[spot], rows.at[b], down_sem.at[b])
        second = pltpu.make_async_copy(up.at[spot], chosen.at[b], up_sem.at[b])
        copies.append((first, second))
    for first, _ in copies:
        first.start()
    for _, second in copies:
        second.start()
    step = acts.shape[0] // half
    inputs[3].wait()
    sides = []
    for side, source in ((0, acts), (1, others)):
        parts = []
        for b in range(half):
            at = side * half + b
            copies[at][0].wait()
            part = lax.dot_general(
                source[b * step : (b + 1) * step, :],
                rows[at],
                (((1,), (1,)), ((), ())),
                preferred_element_type=F32,
            )
            parts.append(part * (lax.div(stored[at], owned) == me).astype(F32))
        sides.append(jnp.concatenate(parts, axis=0))
    shrunk[...] = jnp.concatenate(sides, axis=1)
    for _, second in copies:
        second.wait()


def encode(value, slot):
    count, width = value.shape
    largest = jnp.maximum(jnp.max(jnp.abs(value), axis=1, keepdims=True), 1e-30)
    level = jnp.ceil(jnp.log2(largest) * 4.0)
    factor = jnp.exp2(level * -0.25) * LEVELS
    coded = jnp.round(jnp.clip(value * factor, -32767.0, 32767.0))
    coded = coded.astype(jnp.int32).astype(jnp.int16)
    for i in range(count // ROWS):
        slot[:, i * width : (i + 1) * width] = coded[i * ROWS : (i + 1) * ROWS, :]
    row = jnp.sum(jnp.where(diagonal(count), level, 0.0), axis=0, keepdims=True)
    tail = count // ROWS * width
    slot[:, tail : tail + TAIL] = (
        jnp.broadcast_to(row, (ROWS, TAIL)).astype(jnp.int32).astype(jnp.int16)
    )


def diagonal(count):
    shape = (count, TAIL)
    return lax.broadcasted_iota(jnp.int32, shape, 0) == lax.broadcasted_iota(jnp.int32, shape, 1)


def decode(slot, width):
    folds = slot.shape[1] // width
    tail = folds * width
    row = slot[:, tail : tail + TAIL].astype(jnp.int32).astype(F32)[0:1, :]
    count = folds * ROWS
    level = jnp.sum(
        jnp.where(diagonal(count), jnp.broadcast_to(row, (count, TAIL)), 0.0), axis=1, keepdims=True
    )
    values = jnp.concatenate(
        [slot[:, i * width : (i + 1) * width].astype(jnp.int32).astype(F32) for i in range(folds)],
        axis=0,
    )
    return values * (jnp.exp2(level * 0.25) * (1.0 / LEVELS))


def main_kernel(*refs):
    z = lax.div(lax.axis_index("tensor"), 2)
    edge = jnp.logical_or(z == 0, z == 3)

    @pl.when(edge)
    def _():
        run(True, z, *refs)

    @pl.when(jnp.logical_not(edge))
    def _():
        run(False, z, *refs)


def run(
    edge, z,
    acts, matrix, shrunk, chosen, names, out,
    weights, x_out, x_in, z_out, z_in, s_pair, s_sum, s_in, total, d_out, d_in,
    w_sem, x_send, x_recv, z_send, z_recv, s_send, s_recv, d_send, d_recv,
):
    g = lax.axis_index("groups")
    r = lax.axis_index("replica")
    t = lax.axis_index("tensor")
    x = lax.rem(t, 2)
    width = out.shape[1]
    if edge:
        near = 1 + lax.div(z, 3)
        order = [3 - near, 3 - z, near, z]
        hops = [near, near, near]
        slots = [0, 1, 2]
    else:
        near = 3 * (z - 1)
        order = [near, 3 - z, 3 - near, z]
        hops = [near, 3 - z, 3 - near]
        slots = [0, 3, 1]

    def peer(at):
        return (g, r, 2 * at + x)

    pair = (g, r, 2 * z + (1 - x))
    twin = (g, 1 - r, t)
    peers = [peer(lax.rem(z + k, 4)) for k in (1, 2, 3)]

    loads = []
    for i in range(4):
        for j, column in enumerate((1 - x, x)):
            place = pl.multiple_of((2 * order[i] + column) * width, width)
            loads.append(
                pltpu.make_async_copy(
                    matrix.at[:, pl.ds(place, width)], weights.at[2 * i + j], w_sem.at[2 * i + j]
                )
            )
    ready = [loads[i] for i in USED]
    for load in ready[:AHEAD]:
        load.start()

    barrier = pltpu.get_barrier_semaphore()
    for device in [pair, twin] + peers:
        pl.semaphore_signal(barrier, inc=1, device_id=device, device_id_type=MESH)
    pl.semaphore_wait(barrier, 5)

    def remote(source, target, one, two, device):
        return pltpu.make_async_remote_copy(
            src_ref=source, dst_ref=target, send_sem=one, recv_sem=two,
            device_id=device, device_id_type=MESH,
        )

    def send(*what):
        copy = remote(*what)
        copy.start()
        return copy

    def product(at):
        loads[at].wait()
        later = USED.index(at) + AHEAD
        if later < len(USED):
            ready[later].start()
        return jnp.dot(acts[...], weights[at], preferred_element_type=F32)

    def arrived(slot):
        remote(z_out.at[0], z_in.at[slot], z_send.at[0], z_recv.at[slot], peers[0]).wait_recv()
        return decode(z_in.at[slot], width)

    s_copies = [send(shrunk, s_pair, s_send.at[3], s_recv.at[3], pair)]
    x_copies = []
    z_copies = []

    def x_step(i):
        encode(product(2 * i), x_out.at[i])
        x_copies.append(send(x_out.at[i], x_in.at[i], x_send.at[i], x_recv.at[i], pair))

    x_step(0)
    x_step(1)
    s_copies[0].wait_recv()
    s_sum[...] = shrunk[...] + s_pair[...]
    for i in range(3):
        s_copies.append(send(s_sum, s_in.at[i], s_send.at[i], s_recv.at[i], peers[i]))
    for i in range(3):
        if i < 2:
            x_step(i + 2)
        mine = product(2 * i + 1)
        x_copies[i].wait_recv()
        mine = mine + decode(x_in.at[i], width)
        if not edge and i:
            mine = mine + arrived(i - 1)
        encode(mine, z_out.at[i])
        z_copies.append(
            send(z_out.at[i], z_in.at[slots[i]], z_send.at[i], z_recv.at[slots[i]], peer(hops[i]))
        )
    total[...] = product(7)

    for copy in s_copies[1:]:
        copy.wait_recv()
    full = s_sum[...] + s_in[0] + s_in[1] + s_in[2]
    high = full.astype(jnp.bfloat16)
    rest = full - high.astype(F32)
    middle = rest.astype(jnp.bfloat16)
    low = (rest - middle.astype(F32)).astype(jnp.bfloat16)
    half = chosen.shape[0] // 2
    rank = chosen.shape[1]
    count = acts.shape[0]
    step = count // half

    def delta(side, b):
        rows = slice(b * step, (b + 1) * step)
        lanes = slice(side * rank, (side + 1) * rank)
        three = jnp.concatenate([high[rows, lanes], middle[rows, lanes], low[rows, lanes]], axis=0)
        got = jnp.dot(three, chosen[side * half + b], preferred_element_type=F32)
        return got[0:step] + got[step : 2 * step] + got[2 * step : 3 * step]

    for b in range(half):
        d_out[b * step : (b + 1) * step, :] = delta(1, b)
    d_copy = send(d_out, d_in, d_send, d_recv, twin)
    same = lax.broadcasted_iota(jnp.int32, (count, count), 0) == lax.broadcasted_iota(
        jnp.int32, (count, count), 1
    )
    named = jnp.broadcast_to((names[...] >= 0).astype(F32), (count, count))
    alive = jnp.sum(jnp.where(same, named, 0.0), axis=1, keepdims=True)
    own = jnp.concatenate([delta(0, b) for b in range(half)], axis=0)
    d_copy.wait_recv()
    total[...] += (own + d_in[...]) * alive
    x_copies[3].wait_recv()
    total[...] += decode(x_in.at[3], width)
    if edge:
        total[...] += arrived(0)
        last = 1
    else:
        total[...] += arrived(2)
        last = 3
    out[...] = (total[...] + arrived(last)).astype(out.dtype)
    for copy in s_copies + x_copies + z_copies + [d_copy]:
        copy.wait_send()


def kernel_shards(
    acts,
    base_output_matrix,
    stored_down_factors,
    stored_up_factors,
    adapter_storage_row,
    adapter_per_block,
    adapter_per_token,
):
    rows, features = acts.shape
    owned, _, rank = stored_down_factors.shape
    width = stored_up_factors.shape[2]
    half = adapter_per_block.shape[0]
    other_blocks = lax.ppermute(adapter_per_block, "replica", [(0, 1), (1, 0)])
    others = lax.ppermute(acts, "replica", [(0, 1), (1, 0)])
    hbm = pl.BlockSpec(memory_space=pltpu.HBM)
    vmem = pl.BlockSpec(memory_space=pltpu.VMEM)
    anywhere = pl.BlockSpec(memory_space=pl.ANY)
    shrunk, chosen = pl.pallas_call(
        functools.partial(pick_kernel, owned),
        out_shape=[
            jax.ShapeDtypeStruct((rows, 2 * rank), F32),
            jax.ShapeDtypeStruct((2 * half, rank, width), jnp.bfloat16),
        ],
        in_specs=[hbm, vmem, hbm, hbm, vmem, anywhere, anywhere],
        out_specs=[vmem, vmem],
        scratch_shapes=[
            pltpu.SMEM(adapter_per_block.shape, jnp.int32),
            pltpu.SMEM(adapter_per_block.shape, jnp.int32),
            pltpu.SMEM(adapter_storage_row.shape, jnp.int32),
            pltpu.VMEM(acts.shape, jnp.bfloat16),
            pltpu.VMEM((2 * half, rank, features), jnp.bfloat16),
            pltpu.SemaphoreType.DMA((4,)),
            pltpu.SemaphoreType.DMA((2 * half,)),
            pltpu.SemaphoreType.DMA((2 * half,)),
        ],
        compiler_params=pltpu.CompilerParams(vmem_limit_bytes=50 * 2**20),
        name="pick",
    )(
        adapter_per_block, other_blocks, adapter_storage_row, acts, others,
        jnp.swapaxes(stored_down_factors, 1, 2), stored_up_factors,
    )
    coded = (ROWS, rows // ROWS * width + TAIL)
    dma = pltpu.SemaphoreType.DMA
    return pl.pallas_call(
        main_kernel,
        out_shape=jax.ShapeDtypeStruct((rows, width), jnp.bfloat16),
        in_specs=[vmem, anywhere, vmem, vmem, vmem],
        out_specs=vmem,
        scratch_shapes=[
            pltpu.VMEM((8, features, width), jnp.bfloat16),
            pltpu.VMEM((4,) + coded, jnp.int16),
            pltpu.VMEM((4,) + coded, jnp.int16),
            pltpu.VMEM((3,) + coded, jnp.int16),
            pltpu.VMEM((4,) + coded, jnp.int16),
            pltpu.VMEM((rows, 2 * rank), F32),
            pltpu.VMEM((rows, 2 * rank), F32),
            pltpu.VMEM((3, rows, 2 * rank), F32),
            pltpu.VMEM((rows, width), F32),
            pltpu.VMEM((rows, width), F32),
            pltpu.VMEM((rows, width), F32),
            dma((8,)), dma((4,)), dma((4,)), dma((3,)), dma((4,)), dma((4,)), dma((4,)), dma, dma,
        ],
        compiler_params=pltpu.CompilerParams(
            collective_id=0, has_side_effects=True, vmem_limit_bytes=50 * 2**20
        ),
        name="main",
    )(acts, base_output_matrix, shrunk, chosen, adapter_per_token.reshape(1, rows))


def shards(
    acts,
    base_output_matrix,
    stored_down_factors,
    stored_up_factors,
    adapter_storage_row,
    adapter_per_block,
    adapter_per_token,
):
    tok_rows, feature_list = acts.shape
    owned = stored_down_factors.shape[0]
    block_count = adapter_per_block.shape[0]
    block_rows = tok_rows // block_count
    wanted = lax.all_gather(adapter_per_block, "replica", axis=0, tiled=True)
    every = lax.all_gather(acts, "replica", axis=0, tiled=True)
    blocks = wanted.shape[0]
    stored = adapter_storage_row[wanted]
    here = (stored // owned == lax.axis_index("replica")).astype(jnp.float32)[:, None, None]
    local = stored % owned
    shrunk_part = jnp.einsum(
        "bkf,bfr->bkr",
        every.reshape(blocks, block_rows, feature_list),
        stored_down_factors[local],
        preferred_element_type=jnp.float32,
    )
    shrunk = lax.psum(shrunk_part * here, "tensor")
    delta_all = jnp.einsum(
        "bkr,brc->bkc",
        shrunk,
        stored_up_factors[local].astype(jnp.float32),
        precision=lax.Precision.HIGHEST,
    )
    delta = lax.psum_scatter(
        delta_all.reshape(blocks * block_rows, -1), "replica", scatter_dimension=0, tiled=True
    )
    part_base = jnp.dot(acts, base_output_matrix, preferred_element_type=jnp.float32)
    base = lax.psum_scatter(part_base, "tensor", scatter_dimension=1, tiled=True)
    alive = (adapter_per_token >= 0)[:, None]
    return (base + jnp.where(alive, delta, 0.0)).astype(jnp.bfloat16)


def solution(mesh):
    placed = (
        P(("groups", "replica"), "tensor"),
        P("tensor", None),
        P("replica", "tensor", None),
        P("replica", None, "tensor"),
        P(),
        P(("groups", "replica")),
        P(("groups", "replica")),
    )
    fits = mesh.shape["tensor"] == 8 and mesh.shape["replica"] == 2
    return jax.shard_map(
        kernel_shards if fits else shards,
        mesh=mesh,
        in_specs=placed,
        out_specs=P(("groups", "replica"), "tensor"),
        check_vma=False,
    )
```

```python
import functools

import jax
import jax.numpy as jnp
from jax import lax
from jax.experimental import pallas as pl
from jax.experimental.pallas import tpu as pltpu
from jax.sharding import PartitionSpec as P

MESH = pl.DeviceIdType.MESH
F32 = jnp.float32
TAIL = 128
LEVELS = 32000.0
ROWS = 16
USED = (0, 2, 4, 1, 6, 3, 5, 7)
AHEAD = 2


def pick_kernel(
    owned, wanted_in, other_in, table_in, acts_in, others, down, up, shrunk, chosen,
    wanted, other_wanted, table, acts, rows, in_sem, down_sem, up_sem,
):
    inputs = [
        pltpu.make_async_copy(source, target, in_sem.at[i])
        for i, (source, target) in enumerate(
            ((wanted_in, wanted), (other_in, other_wanted), (table_in, table), (acts_in, acts))
        )
    ]
    for copy in inputs:
        copy.start()
    for copy in inputs[:3]:
        copy.wait()
    me = lax.axis_index("replica")
    half = wanted.shape[0]
    count = 2 * half
    stored = [table[wanted[b]] for b in range(half)]
    stored += [table[other_wanted[b]] for b in range(half)]
    copies = []
    for b in range(count):
        spot = lax.rem(stored[b], owned)
        first = pltpu.make_async_copy(down.at[spot], rows.at[b], down_sem.at[b])
        second = pltpu.make_async_copy(up.at[spot], chosen.at[b], up_sem.at[b])
        copies.append((first, second))
    for first, _ in copies:
        first.start()
    for _, second in copies:
        second.start()
    step = acts.shape[0] // half
    inputs[3].wait()
    sides = []
    for side, source in ((0, acts), (1, others)):
        parts = []
        for b in range(half):
            at = side * half + b
            copies[at][0].wait()
            part = lax.dot_general(
                source[b * step : (b + 1) * step, :],
                rows[at],
                (((1,), (1,)), ((), ())),
                preferred_element_type=F32,
            )
            parts.append(part * (lax.div(stored[at], owned) == me).astype(F32))
        sides.append(jnp.concatenate(parts, axis=0))
    shrunk[...] = jnp.concatenate(sides, axis=1)
    for _, second in copies:
        second.wait()


def encode(value, slot):
    count, width = value.shape
    largest = jnp.maximum(jnp.max(jnp.abs(value), axis=1, keepdims=True), 1e-30)
    level = jnp.ceil(jnp.log2(largest) * 4.0)
    factor = jnp.exp2(level * -0.25) * LEVELS
    coded = jnp.round(jnp.clip(value * factor, -32767.0, 32767.0))
    coded = coded.astype(jnp.int32).astype(jnp.int16)
    for i in range(count // ROWS):
        slot[:, i * width : (i + 1) * width] = coded[i * ROWS : (i + 1) * ROWS, :]
    row = jnp.sum(jnp.where(diagonal(count), level, 0.0), axis=0, keepdims=True)
    tail = count // ROWS * width
    slot[:, tail : tail + TAIL] = (
        jnp.broadcast_to(row, (ROWS, TAIL)).astype(jnp.int32).astype(jnp.int16)
    )


def diagonal(count):
    shape = (count, TAIL)
    return lax.broadcasted_iota(jnp.int32, shape, 0) == lax.broadcasted_iota(jnp.int32, shape, 1)


def decode(slot, width):
    folds = slot.shape[1] // width
    tail = folds * width
    row = slot[:, tail : tail + TAIL].astype(jnp.int32).astype(F32)[0:1, :]
    count = folds * ROWS
    level = jnp.sum(
        jnp.where(diagonal(count), jnp.broadcast_to(row, (count, TAIL)), 0.0), axis=1, keepdims=True
    )
    values = jnp.concatenate(
        [slot[:, i * width : (i + 1) * width].astype(jnp.int32).astype(F32) for i in range(folds)],
        axis=0,
    )
    return values * (jnp.exp2(level * 0.25) * (1.0 / LEVELS))


def main_kernel(*refs):
    z = lax.div(lax.axis_index("tensor"), 2)
    edge = jnp.logical_or(z == 0, z == 3)

    @pl.when(edge)
    def _():
        run(True, z, *refs)

    @pl.when(jnp.logical_not(edge))
    def _():
        run(False, z, *refs)


def run(
    edge, z,
    acts, matrix, shrunk, chosen, names, out,
    weights, x_out, x_in, z_out, z_in, s_pair, s_sum, s_in, total, d_out, d_in,
    w_sem, x_send, x_recv, z_send, z_recv, s_send, s_recv, d_send, d_recv,
):
    g = lax.axis_index("groups")
    r = lax.axis_index("replica")
    t = lax.axis_index("tensor")
    x = lax.rem(t, 2)
    width = out.shape[1]
    if edge:
        near = 1 + lax.div(z, 3)
        order = [3 - near, 3 - z, near, z]
        hops = [near, near, near]
        slots = [0, 1, 2]
    else:
        near = 3 * (z - 1)
        order = [near, 3 - z, 3 - near, z]
        hops = [near, 3 - z, 3 - near]
        slots = [0, 3, 1]

    def peer(at):
        return (g, r, 2 * at + x)

    pair = (g, r, 2 * z + (1 - x))
    twin = (g, 1 - r, t)
    peers = [peer(lax.rem(z + k, 4)) for k in (1, 2, 3)]

    barrier = pltpu.get_barrier_semaphore()
    for device in [pair, twin] + peers:
        pl.semaphore_signal(barrier, inc=1, device_id=device, device_id_type=MESH)

    loads = []
    for i in range(4):
        for j, column in enumerate((1 - x, x)):
            place = pl.multiple_of((2 * order[i] + column) * width, width)
            loads.append(
                pltpu.make_async_copy(
                    matrix.at[:, pl.ds(place, width)], weights.at[2 * i + j], w_sem.at[2 * i + j]
                )
            )
    ready = [loads[i] for i in USED]
    for load in ready[:AHEAD]:
        load.start()

    def remote(source, target, one, two, device):
        return pltpu.make_async_remote_copy(
            src_ref=source, dst_ref=target, send_sem=one, recv_sem=two,
            device_id=device, device_id_type=MESH,
        )

    def send(*what):
        copy = remote(*what)
        copy.start()
        return copy

    def product(at):
        loads[at].wait()
        later = USED.index(at) + AHEAD
        if later < len(USED):
            ready[later].start()
        return jnp.dot(acts[...], weights[at], preferred_element_type=F32)

    def arrived(slot):
        remote(z_out.at[0], z_in.at[slot], z_send.at[0], z_recv.at[slot], peers[0]).wait_recv()
        return decode(z_in.at[slot], width)

    encode(product(0), x_out.at[0])
    pl.semaphore_wait(barrier, 5)
    s_copies = [send(shrunk, s_pair, s_send.at[3], s_recv.at[3], pair)]
    x_copies = []
    z_copies = []

    def x_step(i):
        if i:
            encode(product(2 * i), x_out.at[i])
        x_copies.append(send(x_out.at[i], x_in.at[i], x_send.at[i], x_recv.at[i], pair))

    x_step(0)
    x_step(1)
    s_copies[0].wait_recv()
    s_sum[...] = shrunk[...] + s_pair[...]
    for i in range(3):
        s_copies.append(send(s_sum, s_in.at[i], s_send.at[i], s_recv.at[i], peers[i]))
    for i in range(3):
        if i < 2:
            x_step(i + 2)
        mine = product(2 * i + 1)
        x_copies[i].wait_recv()
        mine = mine + decode(x_in.at[i], width)
        if not edge and i:
            mine = mine + arrived(i - 1)
        encode(mine, z_out.at[i])
        z_copies.append(
            send(z_out.at[i], z_in.at[slots[i]], z_send.at[i], z_recv.at[slots[i]], peer(hops[i]))
        )
    total[...] = product(7)

    for copy in s_copies[1:]:
        copy.wait_recv()
    full = s_sum[...] + s_in[0] + s_in[1] + s_in[2]
    high = full.astype(jnp.bfloat16)
    rest = full - high.astype(F32)
    middle = rest.astype(jnp.bfloat16)
    low = (rest - middle.astype(F32)).astype(jnp.bfloat16)
    half = chosen.shape[0] // 2
    rank = chosen.shape[1]
    count = acts.shape[0]
    step = count // half

    def delta(side, b):
        rows = slice(b * step, (b + 1) * step)
        lanes = slice(side * rank, (side + 1) * rank)
        three = jnp.concatenate([high[rows, lanes], middle[rows, lanes], low[rows, lanes]], axis=0)
        got = jnp.dot(three, chosen[side * half + b], preferred_element_type=F32)
        return got[0:step] + got[step : 2 * step] + got[2 * step : 3 * step]

    for b in range(half):
        d_out[b * step : (b + 1) * step, :] = delta(1, b)
    d_copy = send(d_out, d_in, d_send, d_recv, twin)
    same = lax.broadcasted_iota(jnp.int32, (count, count), 0) == lax.broadcasted_iota(
        jnp.int32, (count, count), 1
    )
    named = jnp.broadcast_to((names[...] >= 0).astype(F32), (count, count))
    alive = jnp.sum(jnp.where(same, named, 0.0), axis=1, keepdims=True)
    own = jnp.concatenate([delta(0, b) for b in range(half)], axis=0)
    d_copy.wait_recv()
    total[...] += (own + d_in[...]) * alive
    x_copies[3].wait_recv()
    total[...] += decode(x_in.at[3], width)
    if edge:
        total[...] += arrived(0)
        last = 1
    else:
        total[...] += arrived(2)
        last = 3
    out[...] = (total[...] + arrived(last)).astype(out.dtype)
    for copy in s_copies + x_copies + z_copies + [d_copy]:
        copy.wait_send()


def kernel_shards(
    acts,
    base_output_matrix,
    stored_down_factors,
    stored_up_factors,
    adapter_storage_row,
    adapter_per_block,
    adapter_per_token,
):
    rows, features = acts.shape
    owned, _, rank = stored_down_factors.shape
    width = stored_up_factors.shape[2]
    half = adapter_per_block.shape[0]
    other_blocks = lax.ppermute(adapter_per_block, "replica", [(0, 1), (1, 0)])
    others = lax.ppermute(acts, "replica", [(0, 1), (1, 0)])
    hbm = pl.BlockSpec(memory_space=pltpu.HBM)
    vmem = pl.BlockSpec(memory_space=pltpu.VMEM)
    anywhere = pl.BlockSpec(memory_space=pl.ANY)
    shrunk, chosen = pl.pallas_call(
        functools.partial(pick_kernel, owned),
        out_shape=[
            jax.ShapeDtypeStruct((rows, 2 * rank), F32),
            jax.ShapeDtypeStruct((2 * half, rank, width), jnp.bfloat16),
        ],
        in_specs=[hbm, vmem, hbm, hbm, vmem, anywhere, anywhere],
        out_specs=[vmem, vmem],
        scratch_shapes=[
            pltpu.SMEM(adapter_per_block.shape, jnp.int32),
            pltpu.SMEM(adapter_per_block.shape, jnp.int32),
            pltpu.SMEM(adapter_storage_row.shape, jnp.int32),
            pltpu.VMEM(acts.shape, jnp.bfloat16),
            pltpu.VMEM((2 * half, rank, features), jnp.bfloat16),
            pltpu.SemaphoreType.DMA((4,)),
            pltpu.SemaphoreType.DMA((2 * half,)),
            pltpu.SemaphoreType.DMA((2 * half,)),
        ],
        compiler_params=pltpu.CompilerParams(vmem_limit_bytes=50 * 2**20),
        name="pick",
    )(
        adapter_per_block, other_blocks, adapter_storage_row, acts, others,
        jnp.swapaxes(stored_down_factors, 1, 2), stored_up_factors,
    )
    coded = (ROWS, rows // ROWS * width + TAIL)
    dma = pltpu.SemaphoreType.DMA
    return pl.pallas_call(
        main_kernel,
        out_shape=jax.ShapeDtypeStruct((rows, width), jnp.bfloat16),
        in_specs=[vmem, anywhere, vmem, vmem, vmem],
        out_specs=vmem,
        scratch_shapes=[
            pltpu.VMEM((8, features, width), jnp.bfloat16),
            pltpu.VMEM((4,) + coded, jnp.int16),
            pltpu.VMEM((4,) + coded, jnp.int16),
            pltpu.VMEM((3,) + coded, jnp.int16),
            pltpu.VMEM((4,) + coded, jnp.int16),
            pltpu.VMEM((rows, 2 * rank), F32),
            pltpu.VMEM((rows, 2 * rank), F32),
            pltpu.VMEM((3, rows, 2 * rank), F32),
            pltpu.VMEM((rows, width), F32),
            pltpu.VMEM((rows, width), F32),
            pltpu.VMEM((rows, width), F32),
            dma((8,)), dma((4,)), dma((4,)), dma((3,)), dma((4,)), dma((4,)), dma((4,)), dma, dma,
        ],
        compiler_params=pltpu.CompilerParams(
            collective_id=0, has_side_effects=True, vmem_limit_bytes=50 * 2**20
        ),
        name="main",
    )(acts, base_output_matrix, shrunk, chosen, adapter_per_token.reshape(1, rows))


def shards(
    acts,
    base_output_matrix,
    stored_down_factors,
    stored_up_factors,
    adapter_storage_row,
    adapter_per_block,
    adapter_per_token,
):
    tok_rows, feature_list = acts.shape
    owned = stored_down_factors.shape[0]
    block_count = adapter_per_block.shape[0]
    block_rows = tok_rows // block_count
    wanted = lax.all_gather(adapter_per_block, "replica", axis=0, tiled=True)
    every = lax.all_gather(acts, "replica", axis=0, tiled=True)
    blocks = wanted.shape[0]
    stored = adapter_storage_row[wanted]
    here = (stored // owned == lax.axis_index("replica")).astype(jnp.float32)[:, None, None]
    local = stored % owned
    shrunk_part = jnp.einsum(
        "bkf,bfr->bkr",
        every.reshape(blocks, block_rows, feature_list),
        stored_down_factors[local],
        preferred_element_type=jnp.float32,
    )
    shrunk = lax.psum(shrunk_part * here, "tensor")
    delta_all = jnp.einsum(
        "bkr,brc->bkc",
        shrunk,
        stored_up_factors[local].astype(jnp.float32),
        precision=lax.Precision.HIGHEST,
    )
    delta = lax.psum_scatter(
        delta_all.reshape(blocks * block_rows, -1), "replica", scatter_dimension=0, tiled=True
    )
    part_base = jnp.dot(acts, base_output_matrix, preferred_element_type=jnp.float32)
    base = lax.psum_scatter(part_base, "tensor", scatter_dimension=1, tiled=True)
    alive = (adapter_per_token >= 0)[:, None]
    return (base + jnp.where(alive, delta, 0.0)).astype(jnp.bfloat16)


def solution(mesh):
    placed = (
        P(("groups", "replica"), "tensor"),
        P("tensor", None),
        P("replica", "tensor", None),
        P("replica", None, "tensor"),
        P(),
        P(("groups", "replica")),
        P(("groups", "replica")),
    )
    fits = mesh.shape["tensor"] == 8 and mesh.shape["replica"] == 2
    return jax.shard_map(
        kernel_shards if fits else shards,
        mesh=mesh,
        in_specs=placed,
        out_specs=P(("groups", "replica"), "tensor"),
        check_vma=False,
    )
```

```python
import functools

import jax
import jax.numpy as jnp
from jax import lax
from jax.experimental import pallas as pl
from jax.experimental.pallas import tpu as pltpu
from jax.sharding import PartitionSpec as P

MESH = pl.DeviceIdType.MESH
F32 = jnp.float32
TAIL = 128
LEVELS = 32000.0
ROWS = 16
USED = (0, 2, 4, 6, 1, 3, 5, 7)
AHEAD = 2


def pick_kernel(
    owned, wanted_in, other_in, table_in, acts_in, others, down, up, shrunk, chosen,
    wanted, other_wanted, table, acts, rows, in_sem, down_sem, up_sem,
):
    inputs = [
        pltpu.make_async_copy(source, target, in_sem.at[i])
        for i, (source, target) in enumerate(
            ((wanted_in, wanted), (other_in, other_wanted), (table_in, table), (acts_in, acts))
        )
    ]
    for copy in inputs:
        copy.start()
    for copy in inputs[:3]:
        copy.wait()
    me = lax.axis_index("replica")
    half = wanted.shape[0]
    count = 2 * half
    stored = [table[wanted[b]] for b in range(half)]
    stored += [table[other_wanted[b]] for b in range(half)]
    copies = []
    for b in range(count):
        spot = lax.rem(stored[b], owned)
        first = pltpu.make_async_copy(down.at[spot], rows.at[b], down_sem.at[b])
        second = pltpu.make_async_copy(up.at[spot], chosen.at[b], up_sem.at[b])
        copies.append((first, second))
    for first, _ in copies:
        first.start()
    for _, second in copies:
        second.start()
    step = acts.shape[0] // half
    inputs[3].wait()
    sides = []
    for side, source in ((0, acts), (1, others)):
        parts = []
        for b in range(half):
            at = side * half + b
            copies[at][0].wait()
            part = lax.dot_general(
                source[b * step : (b + 1) * step, :],
                rows[at],
                (((1,), (1,)), ((), ())),
                preferred_element_type=F32,
            )
            parts.append(part * (lax.div(stored[at], owned) == me).astype(F32))
        sides.append(jnp.concatenate(parts, axis=0))
    shrunk[...] = jnp.concatenate(sides, axis=1)
    for _, second in copies:
        second.wait()


def encode(value, slot):
    count, width = value.shape
    largest = jnp.maximum(jnp.max(jnp.abs(value), axis=1, keepdims=True), 1e-30)
    level = jnp.ceil(jnp.log2(largest) * 4.0)
    factor = jnp.exp2(level * -0.25) * LEVELS
    coded = jnp.round(jnp.clip(value * factor, -32767.0, 32767.0))
    coded = coded.astype(jnp.int32).astype(jnp.int16)
    for i in range(count // ROWS):
        slot[:, i * width : (i + 1) * width] = coded[i * ROWS : (i + 1) * ROWS, :]
    row = jnp.sum(jnp.where(diagonal(count), level, 0.0), axis=0, keepdims=True)
    tail = count // ROWS * width
    slot[:, tail : tail + TAIL] = (
        jnp.broadcast_to(row, (ROWS, TAIL)).astype(jnp.int32).astype(jnp.int16)
    )


def diagonal(count):
    shape = (count, TAIL)
    return lax.broadcasted_iota(jnp.int32, shape, 0) == lax.broadcasted_iota(jnp.int32, shape, 1)


def decode(slot, width):
    folds = slot.shape[1] // width
    tail = folds * width
    row = slot[:, tail : tail + TAIL].astype(jnp.int32).astype(F32)[0:1, :]
    count = folds * ROWS
    level = jnp.sum(
        jnp.where(diagonal(count), jnp.broadcast_to(row, (count, TAIL)), 0.0), axis=1, keepdims=True
    )
    values = jnp.concatenate(
        [slot[:, i * width : (i + 1) * width].astype(jnp.int32).astype(F32) for i in range(folds)],
        axis=0,
    )
    return values * (jnp.exp2(level * 0.25) * (1.0 / LEVELS))


def main_kernel(*refs):
    z = lax.div(lax.axis_index("tensor"), 2)
    edge = jnp.logical_or(z == 0, z == 3)

    @pl.when(edge)
    def _():
        run(True, z, *refs)

    @pl.when(jnp.logical_not(edge))
    def _():
        run(False, z, *refs)


def run(
    edge, z,
    acts, matrix, shrunk, chosen, names, out,
    weights, x_out, x_in, z_out, z_in, s_pair, s_sum, s_in, total, d_out, d_in,
    w_sem, x_send, x_recv, z_send, z_recv, s_send, s_recv, d_send, d_recv,
):
    g = lax.axis_index("groups")
    r = lax.axis_index("replica")
    t = lax.axis_index("tensor")
    x = lax.rem(t, 2)
    width = out.shape[1]
    if edge:
        near = 1 + lax.div(z, 3)
        order = [3 - near, 3 - z, near, z]
        hops = [near, near, near]
        slots = [0, 1, 2]
    else:
        near = 3 * (z - 1)
        order = [near, 3 - z, 3 - near, z]
        hops = [near, 3 - z, 3 - near]
        slots = [0, 3, 1]

    def peer(at):
        return (g, r, 2 * at + x)

    pair = (g, r, 2 * z + (1 - x))
    twin = (g, 1 - r, t)
    peers = [peer(lax.rem(z + k, 4)) for k in (1, 2, 3)]

    loads = []
    for i in range(4):
        for j, column in enumerate((1 - x, x)):
            place = pl.multiple_of((2 * order[i] + column) * width, width)
            loads.append(
                pltpu.make_async_copy(
                    matrix.at[:, pl.ds(place, width)], weights.at[2 * i + j], w_sem.at[2 * i + j]
                )
            )
    ready = [loads[i] for i in USED]
    for load in ready[:AHEAD]:
        load.start()

    barrier = pltpu.get_barrier_semaphore()
    for device in [pair, twin] + peers:
        pl.semaphore_signal(barrier, inc=1, device_id=device, device_id_type=MESH)
    pl.semaphore_wait(barrier, 5)

    def remote(source, target, one, two, device):
        return pltpu.make_async_remote_copy(
            src_ref=source, dst_ref=target, send_sem=one, recv_sem=two,
            device_id=device, device_id_type=MESH,
        )

    def send(*what):
        copy = remote(*what)
        copy.start()
        return copy

    def product(at):
        loads[at].wait()
        later = USED.index(at) + AHEAD
        if later < len(USED):
            ready[later].start()
        return jnp.dot(acts[...], weights[at], preferred_element_type=F32)

    def arrived(slot):
        remote(z_out.at[0], z_in.at[slot], z_send.at[0], z_recv.at[slot], peers[0]).wait_recv()
        return decode(z_in.at[slot], width)

    s_copies = [send(shrunk, s_pair, s_send.at[3], s_recv.at[3], pair)]
    x_copies = []
    z_copies = []

    def x_step(i):
        encode(product(2 * i), x_out.at[i])
        x_copies.append(send(x_out.at[i], x_in.at[i], x_send.at[i], x_recv.at[i], pair))

    x_step(0)
    x_step(1)
    s_copies[0].wait_recv()
    s_sum[...] = shrunk[...] + s_pair[...]
    for i in range(3):
        s_copies.append(send(s_sum, s_in.at[i], s_send.at[i], s_recv.at[i], peers[i]))
    x_step(2)
    x_step(3)
    for i in range(3):
        mine = product(2 * i + 1)
        x_copies[i].wait_recv()
        mine = mine + decode(x_in.at[i], width)
        if not edge and i:
            mine = mine + arrived(i - 1)
        encode(mine, z_out.at[i])
        z_copies.append(
            send(z_out.at[i], z_in.at[slots[i]], z_send.at[i], z_recv.at[slots[i]], peer(hops[i]))
        )
    total[...] = product(7)

    for copy in s_copies[1:]:
        copy.wait_recv()
    full = s_sum[...] + s_in[0] + s_in[1] + s_in[2]
    high = full.astype(jnp.bfloat16)
    rest = full - high.astype(F32)
    middle = rest.astype(jnp.bfloat16)
    low = (rest - middle.astype(F32)).astype(jnp.bfloat16)
    half = chosen.shape[0] // 2
    rank = chosen.shape[1]
    count = acts.shape[0]
    step = count // half

    def delta(side, b):
        rows = slice(b * step, (b + 1) * step)
        lanes = slice(side * rank, (side + 1) * rank)
        three = jnp.concatenate([high[rows, lanes], middle[rows, lanes], low[rows, lanes]], axis=0)
        got = jnp.dot(three, chosen[side * half + b], preferred_element_type=F32)
        return got[0:step] + got[step : 2 * step] + got[2 * step : 3 * step]

    for b in range(half):
        d_out[b * step : (b + 1) * step, :] = delta(1, b)
    d_copy = send(d_out, d_in, d_send, d_recv, twin)
    same = lax.broadcasted_iota(jnp.int32, (count, count), 0) == lax.broadcasted_iota(
        jnp.int32, (count, count), 1
    )
    named = jnp.broadcast_to((names[...] >= 0).astype(F32), (count, count))
    alive = jnp.sum(jnp.where(same, named, 0.0), axis=1, keepdims=True)
    own = jnp.concatenate([delta(0, b) for b in range(half)], axis=0)
    d_copy.wait_recv()
    total[...] += (own + d_in[...]) * alive
    x_copies[3].wait_recv()
    total[...] += decode(x_in.at[3], width)
    if edge:
        total[...] += arrived(0)
        last = 1
    else:
        total[...] += arrived(2)
        last = 3
    out[...] = (total[...] + arrived(last)).astype(out.dtype)
    for copy in s_copies + x_copies + z_copies + [d_copy]:
        copy.wait_send()


def kernel_shards(
    acts,
    base_output_matrix,
    stored_down_factors,
    stored_up_factors,
    adapter_storage_row,
    adapter_per_block,
    adapter_per_token,
):
    rows, features = acts.shape
    owned, _, rank = stored_down_factors.shape
    width = stored_up_factors.shape[2]
    half = adapter_per_block.shape[0]
    other_blocks = lax.ppermute(adapter_per_block, "replica", [(0, 1), (1, 0)])
    others = lax.ppermute(acts, "replica", [(0, 1), (1, 0)])
    hbm = pl.BlockSpec(memory_space=pltpu.HBM)
    vmem = pl.BlockSpec(memory_space=pltpu.VMEM)
    anywhere = pl.BlockSpec(memory_space=pl.ANY)
    shrunk, chosen = pl.pallas_call(
        functools.partial(pick_kernel, owned),
        out_shape=[
            jax.ShapeDtypeStruct((rows, 2 * rank), F32),
            jax.ShapeDtypeStruct((2 * half, rank, width), jnp.bfloat16),
        ],
        in_specs=[hbm, vmem, hbm, hbm, vmem, anywhere, anywhere],
        out_specs=[vmem, vmem],
        scratch_shapes=[
            pltpu.SMEM(adapter_per_block.shape, jnp.int32),
            pltpu.SMEM(adapter_per_block.shape, jnp.int32),
            pltpu.SMEM(adapter_storage_row.shape, jnp.int32),
            pltpu.VMEM(acts.shape, jnp.bfloat16),
            pltpu.VMEM((2 * half, rank, features), jnp.bfloat16),
            pltpu.SemaphoreType.DMA((4,)),
            pltpu.SemaphoreType.DMA((2 * half,)),
            pltpu.SemaphoreType.DMA((2 * half,)),
        ],
        compiler_params=pltpu.CompilerParams(vmem_limit_bytes=50 * 2**20),
        name="pick",
    )(
        adapter_per_block, other_blocks, adapter_storage_row, acts, others,
        jnp.swapaxes(stored_down_factors, 1, 2), stored_up_factors,
    )
    coded = (ROWS, rows // ROWS * width + TAIL)
    dma = pltpu.SemaphoreType.DMA
    return pl.pallas_call(
        main_kernel,
        out_shape=jax.ShapeDtypeStruct((rows, width), jnp.bfloat16),
        in_specs=[vmem, anywhere, vmem, vmem, vmem],
        out_specs=vmem,
        scratch_shapes=[
            pltpu.VMEM((8, features, width), jnp.bfloat16),
            pltpu.VMEM((4,) + coded, jnp.int16),
            pltpu.VMEM((4,) + coded, jnp.int16),
            pltpu.VMEM((3,) + coded, jnp.int16),
            pltpu.VMEM((4,) + coded, jnp.int16),
            pltpu.VMEM((rows, 2 * rank), F32),
            pltpu.VMEM((rows, 2 * rank), F32),
            pltpu.VMEM((3, rows, 2 * rank), F32),
            pltpu.VMEM((rows, width), F32),
            pltpu.VMEM((rows, width), F32),
            pltpu.VMEM((rows, width), F32),
            dma((8,)), dma((4,)), dma((4,)), dma((3,)), dma((4,)), dma((4,)), dma((4,)), dma, dma,
        ],
        compiler_params=pltpu.CompilerParams(
            collective_id=0, has_side_effects=True, vmem_limit_bytes=50 * 2**20
        ),
        name="main",
    )(acts, base_output_matrix, shrunk, chosen, adapter_per_token.reshape(1, rows))


def shards(
    acts,
    base_output_matrix,
    stored_down_factors,
    stored_up_factors,
    adapter_storage_row,
    adapter_per_block,
    adapter_per_token,
):
    tok_rows, feature_list = acts.shape
    owned = stored_down_factors.shape[0]
    block_count = adapter_per_block.shape[0]
    block_rows = tok_rows // block_count
    wanted = lax.all_gather(adapter_per_block, "replica", axis=0, tiled=True)
    every = lax.all_gather(acts, "replica", axis=0, tiled=True)
    blocks = wanted.shape[0]
    stored = adapter_storage_row[wanted]
    here = (stored // owned == lax.axis_index("replica")).astype(jnp.float32)[:, None, None]
    local = stored % owned
    shrunk_part = jnp.einsum(
        "bkf,bfr->bkr",
        every.reshape(blocks, block_rows, feature_list),
        stored_down_factors[local],
        preferred_element_type=jnp.float32,
    )
    shrunk = lax.psum(shrunk_part * here, "tensor")
    delta_all = jnp.einsum(
        "bkr,brc->bkc",
        shrunk,
        stored_up_factors[local].astype(jnp.float32),
        precision=lax.Precision.HIGHEST,
    )
    delta = lax.psum_scatter(
        delta_all.reshape(blocks * block_rows, -1), "replica", scatter_dimension=0, tiled=True
    )
    part_base = jnp.dot(acts, base_output_matrix, preferred_element_type=jnp.float32)
    base = lax.psum_scatter(part_base, "tensor", scatter_dimension=1, tiled=True)
    alive = (adapter_per_token >= 0)[:, None]
    return (base + jnp.where(alive, delta, 0.0)).astype(jnp.bfloat16)


def solution(mesh):
    placed = (
        P(("groups", "replica"), "tensor"),
        P("tensor", None),
        P("replica", "tensor", None),
        P("replica", None, "tensor"),
        P(),
        P(("groups", "replica")),
        P(("groups", "replica")),
    )
    fits = mesh.shape["tensor"] == 8 and mesh.shape["replica"] == 2
    return jax.shard_map(
        kernel_shards if fits else shards,
        mesh=mesh,
        in_specs=placed,
        out_specs=P(("groups", "replica"), "tensor"),
        check_vma=False,
    )
```
